32 devices in a mesh: space: 8 (over z, x), band: 4 (over y, core).
Axes of the slice: x: 2, y: 2, z: 4, core: 2. Of those that a mesh axis runs over, the one named last changes fastest.
Arguments:
- orbitals: float32 [96, 512, 256], P('space', 'band'), may hold values from -6 to 6
- potential: float32 [96, 256], P('space'), may hold values from -10 to 10
Outputs:
- rotated: float32 [96, 512, 256], P('space', 'band')
- correlation: float32 [512, 512], replicated
The draws below stay inside these ranges and needn't reach their ends.
All inputs are finite; a program needn't handle non-finite values.
Results may differ from the reference program's by a relative error of at most 0.000098.
Values sent between devices are 32-bit elements; how exact they have to be, the bound alone decides.
A program may use at most 320 MiB of HBM per device.

```python
import jax
import jax.numpy as jnp
from jax import lax

NX = 16
NY = 16
NB = 512
NZ = 96


def draw_orbitals(key, part):
    cells = NX * NY
    shared = jax.random.truncated_normal(jax.random.fold_in(key, 2), -4.0, 4.0, (NZ, 1, cells), jnp.float32)
    signs = 2.0 * jax.random.randint(jax.random.fold_in(key, 3), (1, NB, 1), 0, 2).astype(jnp.float32) - 1.0
    noise = jax.random.truncated_normal(jax.random.fold_in(key, 1), -4.0, 4.0, (NZ, NB, cells), jnp.float32)
    amount = 1.0 / 3.0
    return noise + amount * signs * shared


def level_of(rng, shape, pieces, smallest, high):
    level, own = 1.0, jax.random.fold_in(rng, 6)
    for position, shards_of in pieces:
        draws = jnp.exp(jax.random.uniform(jax.random.fold_in(own, position), (shards_of,), jnp.float32, smallest / len(pieces), high / len(pieces)))
        level = level * jnp.repeat(draws, shape[position] // shards_of).reshape([-1 if axis == position else 1 for axis in range(len(shape))])
    return level


def setup_inputs(seed: int = 0) -> dict:
    streams_of = jax.random.split(jax.random.key(seed), 3)
    return {
        "orbitals": draw_orbitals(jax.random.fold_in(streams_of[2], 71), 0),
        "potential": jnp.clip(jax.random.uniform(streams_of[1], (NZ, NX * NY), jnp.float32, -10.0, 10.0) * level_of(streams_of[1], (NZ, NX * NY), ((0, 8),), -0.4, 0.0), -10.0, 10.0),
    }


COEFS = [12.0 / 7.0, -15.0 / 56.0, 10.0 / 189.0, -1.0 / 112.0, 2.0 / 1925.0, -1.0 / 16632.0]
CENTER_COEF = -5369.0 / 1800.0
INV_SPACING2 = 6.25
SHIFT_MID = 42.0
HALF_SPAN = 38.0

def operate(field, potential):
    grid = field.reshape(NZ, NB, NX, NY)
    lap = 3.0 * CENTER_COEF * grid
    for k in range(6):
        for axis_num in (0, 2, 3):
            lap = lap + COEFS[k] * (jnp.roll(grid, k + 1, axis_num) + jnp.roll(grid, -(k + 1), axis_num))
    lap = lap.reshape(field.shape)
    return -0.5 * INV_SPACING2 * lap + potential[:, None, :] * field

def reference(orbitals, potential):
    first = (operate(orbitals, potential) - SHIFT_MID * orbitals) / HALF_SPAN
    second = 2.0 * (operate(first, potential) - SHIFT_MID * first) / HALF_SPAN - orbitals
    gram = jnp.einsum('zig,zjg->ij', second, second, precision=lax.Precision.HIGHEST)
    correlation = gram / float(NX * NY * NZ)
    lower = jnp.linalg.cholesky(correlation)
    ident = jnp.eye(NB, dtype=jnp.float32)
    factor = jax.scipy.linalg.solve_triangular(lower, ident, lower=True).T
    rotated = jnp.einsum('zig,ij->zjg', second, factor, precision=lax.Precision.HIGHEST)
    return (rotated, correlation)
```

```python
import jax
import jax.numpy as jnp
import numpy as np
from jax import lax
from jax.sharding import PartitionSpec as P
from jax.experimental import pallas as pl
from jax.experimental.pallas import tpu as pltpu

EXACT = lax.Precision.HIGHEST
BLOCK = 128
ROWS = 8


def factor_block(tile, spread):
    shape = (ROWS, BLOCK)
    lane = lax.broadcasted_iota(jnp.int32, shape, 1)
    row = lax.broadcasted_iota(jnp.int32, shape, 0)
    groups = BLOCK // ROWS
    for t in range(groups):
        base = t * ROWS
        inside = (lane >= base) & (lane < base + ROWS)
        panel = tile[base : base + ROWS, :]
        below = [tile[g * ROWS : (g + 1) * ROWS, :] for g in range(t + 1, groups)]
        cols = [
            [jnp.broadcast_to(block[:, base + j : base + j + 1], shape) for j in range(ROWS)]
            for block in below
        ]
        for j in range(ROWS):
            spread[j * ROWS : (j + 1) * ROWS, :] = jnp.broadcast_to(
                panel[:, base + j : base + j + 1], shape
            )
        tile[base : base + ROWS, :] = jnp.where(
            inside, jnp.where(lane == base + row, 1.0, 0.0), panel
        )
        below = [jnp.where(inside, 0.0, block) for block in below]
        own = {}
        for j in range(ROWS):
            for i in range(j, ROWS):
                own[i, j] = jnp.broadcast_to(spread[j * ROWS + i : j * ROWS + i + 1, :], shape)
        line = [
            jnp.broadcast_to(tile[base + j : base + j + 1, :], shape) for j in range(ROWS)
        ]
        for j in range(ROWS):
            scale = lax.rsqrt(own[j, j])
            line[j] = line[j] * scale
            for i in range(j + 1, ROWS):
                own[i, j] = own[i, j] * scale
            for i in range(j + 1, ROWS):
                for k in range(j + 1, i + 1):
                    own[i, k] = own[i, k] - own[i, j] * own[k, j]
                line[i] = line[i] - own[i, j] * line[j]
            for g in range(len(below)):
                cols[g][j] = cols[g][j] * scale
                for k in range(j + 1, ROWS):
                    cols[g][k] = cols[g][k] - cols[g][j] * own[k, j]
                below[g] = below[g] - cols[g][j] * line[j]
        for j in range(ROWS):
            tile[base + j : base + j + 1, :] = line[j][0:1, :]
        for g in range(len(below)):
            start = (t + 1 + g) * ROWS
            tile[start : start + ROWS, :] = below[g]


def inverse_factor_kernel(s_ref, w_ref, tile, spread, panel):
    size = s_ref.shape[0]
    blocks = size // BLOCK
    w_ref[...] = s_ref[...]
    lower = lax.broadcasted_iota(jnp.int32, (BLOCK, BLOCK), 0) >= lax.broadcasted_iota(
        jnp.int32, (BLOCK, BLOCK), 1
    )

    def step(k, carry):
        rows = pl.ds(pl.multiple_of(k * BLOCK, BLOCK), BLOCK)
        tile[...] = w_ref[rows, rows]
        factor_block(tile, spread)
        inverse = jnp.where(lower, tile[...], 0.0)
        panel[...] = jnp.dot(
            inverse, w_ref[rows, :], precision=EXACT, preferred_element_type=jnp.float32
        )

        def update(i, carry):
            other = pl.ds(pl.multiple_of(i * BLOCK, BLOCK), BLOCK)
            left = panel[:, other]
            w_ref[other, rows] = jnp.zeros((BLOCK, BLOCK), jnp.float32)
            w_ref[other, :] = w_ref[other, :] - lax.dot_general(
                left,
                panel[...],
                (((0,), (0,)), ((), ())),
                precision=EXACT,
                preferred_element_type=jnp.float32,
            )
            return carry

        keep = [panel[:, c * BLOCK : (c + 1) * BLOCK] for c in range(blocks)]
        for c in range(blocks):
            panel[:, c * BLOCK : (c + 1) * BLOCK] = jnp.where(k == c, inverse, keep[c])
        lax.fori_loop(k + 1, blocks, update, 0)
        w_ref[rows, :] = panel[...]
        return carry

    lax.fori_loop(0, blocks, step, 0)
    for c in range(blocks):
        for r in range(blocks):
            if r < c:
                w_ref[r * BLOCK : (r + 1) * BLOCK, c * BLOCK : (c + 1) * BLOCK] = jnp.zeros(
                    (BLOCK, BLOCK), jnp.float32
                )


def inverse_factor(correlation):
    size = correlation.shape[0]
    return pl.pallas_call(
        inverse_factor_kernel,
        out_shape=jax.ShapeDtypeStruct((size, size), jnp.float32),
        in_specs=[pl.BlockSpec(memory_space=pltpu.VMEM)],
        out_specs=pl.BlockSpec(memory_space=pltpu.VMEM),
        scratch_shapes=[
            pltpu.VMEM((BLOCK, BLOCK), jnp.float32),
            pltpu.VMEM((ROWS * ROWS, BLOCK), jnp.float32),
            pltpu.VMEM((BLOCK, size), jnp.float32),
        ],
        compiler_params=pltpu.CompilerParams(vmem_limit_bytes=32 * 1024 * 1024),
    )(correlation)


COEFS = [12.0 / 7.0, -15.0 / 56.0, 10.0 / 189.0, -1.0 / 112.0, 2.0 / 1925.0, -1.0 / 16632.0]
CENTER_COEF = -5369.0 / 1800.0
INV_SPACING2 = 6.25
SHIFT_MID = 42.0
HALF_SPAN = 38.0
NY = 16


def in_plane_matrix(cells):
    nx = cells // NY
    scale = -0.5 * INV_SPACING2
    full = np.zeros((cells, cells))
    for x in range(nx):
        for y in range(NY):
            at = x * NY + y
            full[at, at] += scale * 3.0 * CENTER_COEF - SHIFT_MID
            for k, coef in enumerate(COEFS):
                for sign in (1, -1):
                    full[((x + sign * (k + 1)) % nx) * NY + y, at] += scale * coef
                    full[x * NY + (y + sign * (k + 1)) % NY, at] += scale * coef
    return full.astype(np.float32)


def padded(block, width, axis):
    count = lax.axis_size(axis)
    forward = [(i, (i + 1) % count) for i in range(count)]
    backward = [(target, source) for source, target in forward]
    low = lax.ppermute(block[-width:], axis, forward)
    high = lax.ppermute(block[:width], axis, backward)
    return jnp.concatenate([low, block, high], axis=0)


def shifted_operator(field, potential, matrix):
    full = padded(field, 6, "space")
    total = full.shape[0]
    out = jnp.einsum("zig,gh->zih", field, matrix, precision=EXACT)
    out = out + potential[:, None, :] * field
    for k in range(6):
        s = k + 1
        pair = full[6 + s : total - 6 + s] + full[6 - s : total - 6 - s]
        out = out + (-0.5 * INV_SPACING2 * COEFS[k]) * pair
    return out


def per_device(orbitals, potential):
    matrix = jnp.asarray(in_plane_matrix(orbitals.shape[2]))
    first = shifted_operator(orbitals, potential, matrix) / HALF_SPAN
    second = 2.0 * shifted_operator(first, potential, matrix) / HALF_SPAN - orbitals
    cells = float(second.shape[0] * lax.axis_size("space") * second.shape[2])
    width = second.shape[1]
    every = lax.all_gather(second, "band", axis=1, tiled=True)
    column_part = jnp.einsum("zig,zjg->ij", every, second, precision=EXACT)
    column_sum = lax.psum(column_part, "space")
    correlation = lax.all_gather(column_sum, "band", axis=1, tiled=True) / cells
    inverse = inverse_factor(correlation)
    own = lax.dynamic_slice_in_dim(inverse, lax.axis_index("band") * width, width, 0)
    rotated = jnp.einsum("zig,ji->zjg", every, own, precision=EXACT)
    return (rotated, correlation)


def solution(mesh):
    return jax.shard_map(
        per_device,
        mesh=mesh,
        in_specs=(P("space", "band", None), P("space", None)),
        out_specs=(P("space", "band", None), P()),
        check_vma=False,
    )
```

```python
import functools
import jax
import jax.numpy as jnp
import numpy as np
from jax import lax
from jax.sharding import PartitionSpec as P
from jax.experimental import pallas as pl
from jax.experimental.pallas import tpu as pltpu

EXACT = lax.Precision.HIGHEST
BLOCK = 128
ROWS = 8


def factor_block(tile, spread):
    shape = (ROWS, BLOCK)
    lane = lax.broadcasted_iota(jnp.int32, shape, 1)
    row = lax.broadcasted_iota(jnp.int32, shape, 0)
    groups = BLOCK // ROWS
    for t in range(groups):
        base = t * ROWS
        inside = (lane >= base) & (lane < base + ROWS)
        panel = tile[base : base + ROWS, :]
        below = [tile[g * ROWS : (g + 1) * ROWS, :] for g in range(t + 1, groups)]
        cols = [
            [jnp.broadcast_to(block[:, base + j : base + j + 1], shape) for j in range(ROWS)]
            for block in below
        ]
        for j in range(ROWS):
            spread[j * ROWS : (j + 1) * ROWS, :] = jnp.broadcast_to(
                panel[:, base + j : base + j + 1], shape
            )
        tile[base : base + ROWS, :] = jnp.where(
            inside, jnp.where(lane == base + row, 1.0, 0.0), panel
        )
        below = [jnp.where(inside, 0.0, block) for block in below]
        own = {}
        for j in range(ROWS):
            for i in range(j, ROWS):
                own[i, j] = jnp.broadcast_to(spread[j * ROWS + i : j * ROWS + i + 1, :], shape)
        line = [
            jnp.broadcast_to(tile[base + j : base + j + 1, :], shape) for j in range(ROWS)
        ]
        for j in range(ROWS):
            scale = lax.rsqrt(own[j, j])
            line[j] = line[j] * scale
            for i in range(j + 1, ROWS):
                own[i, j] = own[i, j] * scale
            for i in range(j + 1, ROWS):
                for k in range(j + 1, i + 1):
                    own[i, k] = own[i, k] - own[i, j] * own[k, j]
                line[i] = line[i] - own[i, j] * line[j]
            for g in range(len(below)):
                cols[g][j] = cols[g][j] * scale
                for k in range(j + 1, ROWS):
                    cols[g][k] = cols[g][k] - cols[g][j] * own[k, j]
                below[g] = below[g] - cols[g][j] * line[j]
        for j in range(ROWS):
            tile[base + j : base + j + 1, :] = line[j][0:1, :]
        for g in range(len(below)):
            start = (t + 1 + g) * ROWS
            tile[start : start + ROWS, :] = below[g]

COEFS = [12.0 / 7.0, -15.0 / 56.0, 10.0 / 189.0, -1.0 / 112.0, 2.0 / 1925.0, -1.0 / 16632.0]
CENTER_COEF = -5369.0 / 1800.0
INV_SPACING2 = 6.25
SHIFT_MID = 42.0
HALF_SPAN = 38.0
NY = 16
REACH = 6
CHUNK = 16
MESH = pl.DeviceIdType.MESH


def in_plane_matrix(cells):
    nx = cells // NY
    scale = -0.5 * INV_SPACING2
    full = np.zeros((cells, cells))
    for x in range(nx):
        for y in range(NY):
            at = x * NY + y
            full[at, at] += scale * 3.0 * CENTER_COEF - SHIFT_MID
            for k, coef in enumerate(COEFS):
                for sign in (1, -1):
                    full[((x + sign * (k + 1)) % nx) * NY + y, at] += scale * coef
                    full[x * NY + (y + sign * (k + 1)) % NY, at] += scale * coef
    return full.astype(np.float32)


def inverse_factor_in(s_ref, w_ref, tile, spread, panel):
    size = s_ref.shape[0]
    blocks = size // BLOCK
    w_ref[...] = s_ref[...]
    lower = lax.broadcasted_iota(jnp.int32, (BLOCK, BLOCK), 0) >= lax.broadcasted_iota(
        jnp.int32, (BLOCK, BLOCK), 1
    )

    def step(k, carry):
        rows = pl.ds(pl.multiple_of(k * BLOCK, BLOCK), BLOCK)
        tile[...] = w_ref[rows, rows]
        factor_block(tile, spread)
        inverse = jnp.where(lower, tile[...], 0.0)
        panel[...] = jnp.dot(
            inverse, w_ref[rows, :], precision=EXACT, preferred_element_type=jnp.float32
        )

        def update(i, carry):
            other = pl.ds(pl.multiple_of(i * BLOCK, BLOCK), BLOCK)
            left = panel[:, other]
            w_ref[other, rows] = jnp.zeros((BLOCK, BLOCK), jnp.float32)
            w_ref[other, :] = w_ref[other, :] - lax.dot_general(
                left,
                panel[...],
                (((0,), (0,)), ((), ())),
                precision=EXACT,
                preferred_element_type=jnp.float32,
            )
            return carry

        keep = [panel[:, c * BLOCK : (c + 1) * BLOCK] for c in range(blocks)]
        for c in range(blocks):
            panel[:, c * BLOCK : (c + 1) * BLOCK] = jnp.where(k == c, inverse, keep[c])
        lax.fori_loop(k + 1, blocks, update, 0)
        w_ref[rows, :] = panel[...]
        return carry

    lax.fori_loop(0, blocks, step, 0)
    for c in range(blocks):
        for r in range(blocks):
            if r < c:
                w_ref[r * BLOCK : (r + 1) * BLOCK, c * BLOCK : (c + 1) * BLOCK] = jnp.zeros(
                    (BLOCK, BLOCK), jnp.float32
                )


def filter_kernel(
    n, nb, cells, o_ref, p_ref, m_ref, every_out, corr_out,
    ext, pot, first, mixed, every, part, inbox, corr,
    own_sem, pot_send, pot_recv, near_send, near_recv, far_send, far_recv,
    chip_send, chip_recv, core_send, core_recv, pass_send, pass_recv,
    rs_send, rs_recv, ag_send, ag_recv,
    cchip_send, cchip_recv, ccore_send, ccore_recv, cpass_send, cpass_recv, out_sem,
):
    nz, width, area = o_ref.shape
    chunks = width // CHUNK
    chips = nb // 2
    s = lax.axis_index("space")
    b = lax.axis_index("band")
    odd = lax.rem(s, 2)
    near = s + 1 - 2 * odd
    far = lax.rem(s + 2 - 4 * odd + n, n)
    chip = b // 2
    core = lax.rem(b, 2)
    mate = b + 1 - 2 * core
    near_slot = 2 * nz * (1 - odd)
    far_slot = 2 * nz * odd

    def space_at(d):
        return lax.rem(s + d + n, n)

    def band_at(d):
        return lax.rem(chip + d + chips, chips) * 2 + core

    barrier = pltpu.get_barrier_semaphore()
    for d in range(1, n):
        pl.semaphore_signal(barrier, inc=1, device_id={"space": space_at(d)}, device_id_type=MESH)
    for d in range(1, chips):
        pl.semaphore_signal(barrier, inc=1, device_id={"band": band_at(d)}, device_id_type=MESH)
    pl.semaphore_signal(barrier, inc=1, device_id={"band": mate}, device_id_type=MESH)
    pl.semaphore_wait(barrier, n - 1 + chips)

    def remote(src, dst, send, recv, target):
        return pltpu.make_async_remote_copy(
            src_ref=src, dst_ref=dst, send_sem=send, recv_sem=recv,
            device_id=target, device_id_type=MESH,
        )

    def rows_of(c):
        return pl.ds(pl.multiple_of(c * CHUNK, CHUNK), CHUNK)

    def near_copy(c):
        return remote(
            o_ref.at[:, rows_of(c), :],
            ext.at[pl.ds(2 * nz * odd, nz), rows_of(c), :],
            near_send.at[c], near_recv.at[c], {"space": near},
        )

    def near_arrival(c):
        spot = ext.at[pl.ds(near_slot, nz), rows_of(c), :]
        return remote(spot, spot, near_send.at[c], near_recv.at[c], {"space": near})

    def far_copy(c):
        return remote(
            ext.at[pl.ds(near_slot, nz), rows_of(c), :],
            ext.at[pl.ds(far_slot, nz), rows_of(c), :],
            far_send.at[c], far_recv.at[c], {"space": far},
        )

    def far_arrival(c):
        spot = ext.at[pl.ds(far_slot, nz), rows_of(c), :]
        return remote(spot, spot, far_send.at[c], far_recv.at[c], {"space": far})

    def block_rows(band, c):
        return pl.ds(pl.multiple_of(band * width + c * CHUNK, CHUNK), CHUNK)

    def chip_copy(d, c):
        spot = every.at[:, block_rows(b, c), :]
        return remote(spot, spot, chip_send.at[d - 1, c], chip_recv.at[d - 1, c], {"band": band_at(d)})

    def core_copy(c):
        spot = every.at[:, block_rows(b, c), :]
        return remote(spot, spot, core_send.at[c], core_recv.at[c], {"band": mate})

    def core_arrival(c):
        spot = every.at[:, block_rows(mate, c), :]
        return remote(spot, spot, core_send.at[c], core_recv.at[c], {"band": mate})

    def pass_copy(d, c):
        spot = every.at[:, block_rows(band_at(-d), c), :]
        return remote(spot, spot, pass_send.at[d - 1, c], pass_recv.at[d - 1, c], {"band": mate})

    def chip_arrival(d, c):
        spot = every.at[:, block_rows(band_at(-d), c), :]
        return remote(spot, spot, chip_send.at[d - 1, c], chip_recv.at[d - 1, c], {"band": band_at(-d)})

    def pass_arrival(d, c):
        other = band_at(-d) + 1 - 2 * core
        spot = every.at[:, block_rows(other, c), :]
        return remote(spot, spot, pass_send.at[d - 1, c], pass_recv.at[d - 1, c], {"band": mate})

    def take_chip(c):
        for d in range(1, chips):
            chip_arrival(d, c).wait_recv()
            pass_copy(d, c).start()

    near_copy(0).start()
    if chunks > 1:
        near_copy(1).start()
    own = pltpu.make_async_copy(o_ref, ext.at[pl.ds(nz, nz)], own_sem)
    own.start()
    up = remote(p_ref, pot.at[pl.ds(0, nz)], pot_send.at[0], pot_recv.at[0], {"space": space_at(1)})
    down = remote(p_ref, pot.at[pl.ds(2 * nz, nz)], pot_send.at[1], pot_recv.at[1], {"space": space_at(-1)})
    up.start()
    down.start()
    pot[nz : 2 * nz] = p_ref[...]

    near_arrival(0).wait_recv()
    far_copy(0).start()
    near_copy(0).wait_send()
    if chunks > 2:
        near_copy(2).start()
    own.wait()
    up.wait_recv()
    down.wait_recv()

    along = [-0.5 * INV_SPACING2 * coef for coef in COEFS]

    def do_chunk(c, carry):
        rows = rows_of(c)

        @pl.when(c + 1 < chunks)
        def _():
            near_arrival(c + 1).wait_recv()
            far_copy(c + 1).start()
            near_copy(c + 1).wait_send()

        @pl.when(c + 3 < chunks)
        def _():
            near_copy(c + 3).start()

        far_arrival(c).wait_recv()

        wide = nz + 2 * REACH
        slab = ext[nz - REACH : 2 * nz + REACH, rows, :].reshape(wide * CHUNK, area)
        mixed[...] = jnp.dot(
            slab, m_ref[...], precision=EXACT, preferred_element_type=jnp.float32
        ).reshape(wide, CHUNK, area)

        def first_plane(f, carry):
            q = f + (nz - REACH)
            total = mixed[f] + pot[q] * ext[q, rows, :]
            for k in range(REACH):
                total = total + along[k] * (ext[q + k + 1, rows, :] + ext[q - k - 1, rows, :])
            first[f] = total * (1.0 / HALF_SPAN)
            return carry

        lax.fori_loop(0, wide, first_plane, 0, unroll=4)

        slab = first[REACH : nz + REACH].reshape(nz * CHUNK, area)
        mixed[0:nz] = jnp.dot(
            slab, m_ref[...], precision=EXACT, preferred_element_type=jnp.float32
        ).reshape(nz, CHUNK, area)

        def second_plane(j, carry):
            f = j + REACH
            total = mixed[j] + pot[j + nz] * first[f]
            for k in range(REACH):
                total = total + along[k] * (first[f + k + 1] + first[f - k - 1])
            every[j, block_rows(b, c), :] = total * (2.0 / HALF_SPAN) - ext[j + nz, rows, :]
            return carry

        lax.fori_loop(0, nz, second_plane, 0, unroll=4)

        for d in range(1, chips):
            chip_copy(d, c).start()
        core_copy(c).start()

        @pl.when(c >= 2)
        def _():
            take_chip(c - 2)

        return carry

    lax.fori_loop(0, chunks, do_chunk, 0)
    if chunks > 1:
        take_chip(chunks - 2)

    def each_chunk(action):
        def run(c, carry):
            action(c)
            return carry

        lax.fori_loop(0, chunks, run, 0)

    total_cols = nb * width
    slice_rows = width // n

    def gram(start, cols):
        def add(z, total):
            mine = every[z, pl.ds(pl.multiple_of(b * width, width), width), :]
            theirs = every[z, pl.ds(start, cols), :]
            return total + lax.dot_general(
                mine, theirs, (((1,), (1,)), ((), ())),
                precision=EXACT, preferred_element_type=jnp.float32,
            )

        total = lax.fori_loop(0, nz, add, jnp.zeros((width, cols), jnp.float32))
        for t in range(n):
            part[t, :, pl.ds(start, cols)] = total[t * slice_rows : (t + 1) * slice_rows, :]

    span = 2 * width
    staged = span % 128 == 0
    each_chunk(lambda c: core_arrival(c).wait_recv())
    if staged:
        gram(pl.multiple_of(chip * span, span), span)
    take_chip(chunks - 1)
    for d in range(1, chips):
        each_chunk(lambda c: pass_arrival(d, c).wait_recv())
        if staged:
            gram(pl.multiple_of(lax.rem(chip - d + chips, chips) * span, span), span)
    if not staged:
        gram(0, total_cols)
    save = pltpu.make_async_copy(every, every_out, out_sem.at[0])
    save.start()

    def rs_copy(d):
        t = space_at(d)
        return remote(part.at[t], inbox.at[d], rs_send.at[d], rs_recv.at[d], {"space": t})

    def ag_copy(d):
        spot = corr.at[b, s]
        return remote(spot, spot, ag_send.at[d], ag_recv.at[d], {"space": space_at(d)})

    def ag_arrival(d):
        spot = corr.at[b, space_at(-d)]
        return remote(spot, spot, ag_send.at[d], ag_recv.at[d], {"space": space_at(d)})

    for d in range(1, n):
        rs_copy(d).start()
    total = part[s]
    for d in range(1, n):
        rs_copy(d).wait_recv()
        total = total + inbox[d]
    corr[b, s] = total / cells
    for d in range(1, n):
        ag_copy(d).start()
    for d in range(1, n):
        ag_arrival(d).wait_recv()

    def cchip_copy(d):
        spot = corr.at[b]
        return remote(spot, spot, cchip_send.at[d - 1], cchip_recv.at[d - 1], {"band": band_at(d)})

    def cchip_arrival(d):
        spot = corr.at[band_at(-d)]
        return remote(spot, spot, cchip_send.at[d - 1], cchip_recv.at[d - 1], {"band": band_at(-d)})

    def cpass_copy(d):
        spot = corr.at[band_at(-d)]
        return remote(spot, spot, cpass_send.at[d - 1], cpass_recv.at[d - 1], {"band": mate})

    def cpass_arrival(d):
        spot = corr.at[band_at(-d) + 1 - 2 * core]
        return remote(spot, spot, cpass_send.at[d - 1], cpass_recv.at[d - 1], {"band": mate})

    ccore = remote(corr.at[b], corr.at[b], ccore_send, ccore_recv, {"band": mate})
    ccore_arrival = remote(corr.at[mate], corr.at[mate], ccore_send, ccore_recv, {"band": mate})
    for d in range(1, chips):
        cchip_copy(d).start()
    ccore.start()
    for d in range(1, chips):
        cchip_arrival(d).wait_recv()
        cpass_copy(d).start()
    ccore_arrival.wait_recv()
    for d in range(1, chips):
        cpass_arrival(d).wait_recv()
    store = pltpu.make_async_copy(corr, corr_out, out_sem.at[1])
    store.start()

    up.wait_send()
    down.wait_send()
    each_chunk(lambda c: far_copy(c).wait_send())
    each_chunk(lambda c: core_copy(c).wait_send())
    for d in range(1, chips):
        each_chunk(lambda c: chip_copy(d, c).wait_send())
        each_chunk(lambda c: pass_copy(d, c).wait_send())
        cchip_copy(d).wait_send()
        cpass_copy(d).wait_send()
    for d in range(1, n):
        rs_copy(d).wait_send()
        ag_copy(d).wait_send()
    ccore.wait_send()
    save.wait()
    store.wait()


def filter_and_correlate(orbitals, potential):
    nz, width, area = orbitals.shape
    n = lax.axis_size("space")
    nb = lax.axis_size("band")
    chunks = width // CHUNK
    chips = nb // 2
    slices = (nb, n, width // n, nb * width)
    dma = pltpu.SemaphoreType.DMA
    f32 = jnp.float32
    hops = max(chips - 1, 1)
    flops = 6 * 2 * nz * width * area * (3 * area + nb * width)
    every, corr = pl.pallas_call(
        functools.partial(filter_kernel, n, nb, float(nz * n * area)),
        out_shape=(
            jax.ShapeDtypeStruct((nz, nb * width, area), f32),
            jax.ShapeDtypeStruct(slices, f32),
        ),
        in_specs=[
            pl.BlockSpec(memory_space=pl.ANY),
            pl.BlockSpec(memory_space=pltpu.VMEM),
            pl.BlockSpec(memory_space=pltpu.VMEM),
        ],
        out_specs=(pl.BlockSpec(memory_space=pl.ANY), pl.BlockSpec(memory_space=pl.ANY)),
        scratch_shapes=[
            pltpu.VMEM((3 * nz, width, area), f32),
            pltpu.VMEM((3 * nz, 1, area), f32),
            pltpu.VMEM((nz + 2 * REACH, CHUNK, area), f32),
            pltpu.VMEM((nz + 2 * REACH, CHUNK, area), f32),
            pltpu.VMEM((nz, nb * width, area), f32),
            pltpu.VMEM(slices[1:], f32),
            pltpu.VMEM(slices[1:], f32),
            pltpu.VMEM(slices, f32),
            dma, dma((2,)), dma((2,)),
            dma((chunks,)), dma((chunks,)), dma((chunks,)), dma((chunks,)),
            dma((hops, chunks)), dma((hops, chunks)),
            dma((chunks,)), dma((chunks,)),
            dma((hops, chunks)), dma((hops, chunks)),
            dma((n,)), dma((n,)), dma((n,)), dma((n,)),
            dma((hops,)), dma((hops,)), dma, dma, dma((hops,)), dma((hops,)), dma((2,)),
        ],
        compiler_params=pltpu.CompilerParams(
            collective_id=0, has_side_effects=True, vmem_limit_bytes=48 * 1024 * 1024
        ),
        cost_estimate=pl.CostEstimate(flops=flops, bytes_accessed=10 * 2**20, transcendentals=0),
    )(orbitals, potential.reshape(nz, 1, area), jnp.asarray(in_plane_matrix(area)))
    return every, corr.reshape(nb * width, nb * width)


def rotate_kernel(
    s_ref, every_ref, corr_out, out_ref, inverse, tile, spread, panel, every, sems
):
    fetch = pltpu.make_async_copy(every_ref, every, sems.at[0])
    fetch.start()
    store = pltpu.make_async_copy(s_ref, corr_out, sems.at[1])
    store.start()
    inverse_factor_in(s_ref, inverse, tile, spread, panel)
    fetch.wait()
    nz, width, _ = out_ref.shape
    b = lax.axis_index("band")

    def plane(z, carry):
        own = inverse[pl.ds(pl.multiple_of(b * width, width), width), :]
        out_ref[z] = jnp.dot(
            own, every[z], precision=EXACT, preferred_element_type=jnp.float32
        )
        return carry

    lax.fori_loop(0, nz, plane, 0)
    store.wait()


def factor_and_rotate(correlation, every, width):
    size = correlation.shape[0]
    nz, _, area = every.shape
    f32 = jnp.float32
    return pl.pallas_call(
        rotate_kernel,
        out_shape=(
            jax.ShapeDtypeStruct((size, size), f32),
            jax.ShapeDtypeStruct((nz, width, area), f32),
        ),
        in_specs=[pl.BlockSpec(memory_space=pltpu.VMEM), pl.BlockSpec(memory_space=pl.ANY)],
        out_specs=(pl.BlockSpec(memory_space=pl.ANY), pl.BlockSpec(memory_space=pltpu.VMEM)),
        scratch_shapes=[
            pltpu.VMEM((size, size), f32),
            pltpu.VMEM((BLOCK, BLOCK), f32),
            pltpu.VMEM((ROWS * ROWS, BLOCK), f32),
            pltpu.VMEM((BLOCK, size), f32),
            pltpu.VMEM((nz, size, area), f32),
            pltpu.SemaphoreType.DMA((2,)),
        ],
        compiler_params=pltpu.CompilerParams(vmem_limit_bytes=48 * 1024 * 1024),
    )(correlation, every)


def per_device(orbitals, potential):
    every, correlation = filter_and_correlate(orbitals, potential)
    correlation, rotated = factor_and_rotate(correlation, every, orbitals.shape[1])
    return (rotated, correlation)


def solution(mesh):
    return jax.shard_map(
        per_device,
        mesh=mesh,
        in_specs=(P("space", "band", None), P("space", None)),
        out_specs=(P("space", "band", None), P()),
        check_vma=False,
    )
```

```python
import functools
import jax
import jax.numpy as jnp
import numpy as np
from jax import lax
from jax.sharding import PartitionSpec as P
from jax.experimental import pallas as pl
from jax.experimental.pallas import tpu as pltpu

EXACT = lax.Precision.HIGHEST
BLOCK = 128
ROWS = 8


def factor_block(tile, spread):
    shape = (ROWS, BLOCK)
    lane = lax.broadcasted_iota(jnp.int32, shape, 1)
    row = lax.broadcasted_iota(jnp.int32, shape, 0)
    groups = BLOCK // ROWS

    def column(block, at):
        return jnp.broadcast_to(block[:, at : at + 1], shape)

    def spread_row(at):
        return jnp.broadcast_to(spread[at : at + 1, :], shape)

    below = [tile[g * ROWS : (g + 1) * ROWS, :] for g in range(groups)]
    ahead = [column(below[0], j) for j in range(ROWS)]
    for t in range(groups):
        base = t * ROWS
        slot = (t % 2) * 2 * ROWS * ROWS
        inside = (lane >= base) & (lane < base + ROWS)
        panel, below = below[0], below[1:]
        for j in range(ROWS):
            spread[slot + j * ROWS : slot + (j + 1) * ROWS, :] = ahead[j]
        cols = [[column(block, base + j) for j in range(ROWS)] for block in below]
        if below:
            ahead = [column(below[0], base + ROWS + j) for j in range(ROWS)]
        tile[base : base + ROWS, :] = jnp.where(
            inside, jnp.where(lane == base + row, 1.0, 0.0), panel
        )
        below = [jnp.where(inside, 0.0, block) for block in below]
        own = {}
        for j in range(ROWS):
            for i in range(j, ROWS):
                own[i, j] = spread_row(slot + j * ROWS + i)
        line = [
            jnp.broadcast_to(tile[base + j : base + j + 1, :], shape) for j in range(ROWS)
        ]
        for j in range(ROWS):
            scale = lax.rsqrt(own[j, j])
            line[j] = line[j] * scale
            for i in range(j + 1, ROWS):
                own[i, j] = own[i, j] * scale
            for i in range(j + 1, ROWS):
                for k in range(j + 1, i + 1):
                    own[i, k] = own[i, k] - own[i, j] * own[k, j]
                line[i] = line[i] - own[i, j] * line[j]
            for g in range(len(below)):
                cols[g][j] = cols[g][j] * scale
                for k in range(j + 1, ROWS):
                    cols[g][k] = cols[g][k] - cols[g][j] * own[k, j]
                below[g] = below[g] - cols[g][j] * line[j]
            if below:
                start = slot + (ROWS + j) * ROWS
                spread[start : start + ROWS, :] = cols[0][j]
                for k in range(ROWS):
                    ahead[k] = ahead[k] - cols[0][j] * spread_row(start + k)
        for j in range(ROWS):
            tile[base + j : base + j + 1, :] = line[j][0:1, :]


def split(value):
    high = value.astype(jnp.bfloat16)
    return high, (value - high.astype(jnp.float32)).astype(jnp.bfloat16)


def plain_dot(left, right):
    return jnp.dot(left, right, preferred_element_type=jnp.float32)


COEFS = [12.0 / 7.0, -15.0 / 56.0, 10.0 / 189.0, -1.0 / 112.0, 2.0 / 1925.0, -1.0 / 16632.0]
CENTER_COEF = -5369.0 / 1800.0
INV_SPACING2 = 6.25
SHIFT_MID = 42.0
HALF_SPAN = 38.0
NY = 16
REACH = 6
CHUNK = 8
MESH = pl.DeviceIdType.MESH


def in_plane_matrix(cells):
    nx = cells // NY
    scale = -0.5 * INV_SPACING2
    full = np.zeros((cells, cells))
    for x in range(nx):
        for y in range(NY):
            at = x * NY + y
            full[at, at] += scale * 3.0 * CENTER_COEF - SHIFT_MID
            for k, coef in enumerate(COEFS):
                for sign in (1, -1):
                    full[((x + sign * (k + 1)) % nx) * NY + y, at] += scale * coef
                    full[x * NY + (y + sign * (k + 1)) % NY, at] += scale * coef
    return full.astype(np.float32)


def inverse_factor_in(s_ref, w_ref, tile, spread, panel):
    size = s_ref.shape[0]
    blocks = size // BLOCK
    w_ref[...] = s_ref[...]
    lower = lax.broadcasted_iota(jnp.int32, (BLOCK, BLOCK), 0) >= lax.broadcasted_iota(
        jnp.int32, (BLOCK, BLOCK), 1
    )

    def step(k, carry):
        rows = pl.ds(pl.multiple_of(k * BLOCK, BLOCK), BLOCK)
        tile[...] = w_ref[rows, rows]
        factor_block(tile, spread)
        inverse = jnp.where(lower, tile[...], 0.0)
        panel[...] = jnp.dot(
            inverse, w_ref[rows, :], precision=EXACT, preferred_element_type=jnp.float32
        )

        def update(i, carry):
            other = pl.ds(pl.multiple_of(i * BLOCK, BLOCK), BLOCK)
            left = panel[:, other]
            w_ref[other, rows] = jnp.zeros((BLOCK, BLOCK), jnp.float32)
            w_ref[other, :] = w_ref[other, :] - lax.dot_general(
                left,
                panel[...],
                (((0,), (0,)), ((), ())),
                precision=EXACT,
                preferred_element_type=jnp.float32,
            )
            return carry

        keep = [panel[:, c * BLOCK : (c + 1) * BLOCK] for c in range(blocks)]
        for c in range(blocks):
            panel[:, c * BLOCK : (c + 1) * BLOCK] = jnp.where(k == c, inverse, keep[c])
        lax.fori_loop(k + 1, blocks, update, 0)
        w_ref[rows, :] = panel[...]
        return carry

    lax.fori_loop(0, blocks, step, 0)
    for c in range(blocks):
        for r in range(blocks):
            if r < c:
                w_ref[r * BLOCK : (r + 1) * BLOCK, c * BLOCK : (c + 1) * BLOCK] = jnp.zeros(
                    (BLOCK, BLOCK), jnp.float32
                )


def filter_kernel(
    n, nb, cells, o_ref, p_hbm, m_hbm, every_out, corr_out, p_ref, m_ref, mh_ref, ml_ref,
    ext, pot, first, mixed, every, part, inbox, corr,
    own_sem, pot_send, pot_recv, near_send, near_recv, far_send, far_recv,
    chip_send, chip_recv, core_send, core_recv, pass_send, pass_recv,
    rs_send, rs_recv, ag_send, ag_recv,
    cchip_send, cchip_recv, ccore_send, ccore_recv, cpass_send, cpass_recv, out_sem,
):
    nz, width, area = o_ref.shape
    chunks = width // CHUNK
    chips = nb // 2
    s = lax.axis_index("space")
    b = lax.axis_index("band")
    odd = lax.rem(s, 2)
    near = s + 1 - 2 * odd
    far = lax.rem(s + 2 - 4 * odd + n, n)
    chip = b // 2
    core = lax.rem(b, 2)
    mate = b + 1 - 2 * core
    near_slot = 2 * nz * (1 - odd)
    far_slot = 2 * nz * odd

    def space_at(d):
        return lax.rem(s + d + n, n)

    def band_at(d):
        return lax.rem(chip + d + chips, chips) * 2 + core

    fetch_p = pltpu.make_async_copy(p_hbm, p_ref, own_sem.at[1])
    fetch_m = pltpu.make_async_copy(m_hbm, m_ref, own_sem.at[2])
    fetch_p.start()
    fetch_m.start()
    barrier = pltpu.get_barrier_semaphore()
    for d in range(1, n):
        pl.semaphore_signal(barrier, inc=1, device_id={"space": space_at(d)}, device_id_type=MESH)
    for d in range(1, chips):
        pl.semaphore_signal(barrier, inc=1, device_id={"band": band_at(d)}, device_id_type=MESH)
    pl.semaphore_signal(barrier, inc=1, device_id={"band": mate}, device_id_type=MESH)
    pl.semaphore_wait(barrier, n - 1 + chips)

    def remote(src, dst, send, recv, target):
        return pltpu.make_async_remote_copy(
            src_ref=src, dst_ref=dst, send_sem=send, recv_sem=recv,
            device_id=target, device_id_type=MESH,
        )

    def rows_of(c):
        return pl.ds(pl.multiple_of(c * CHUNK, CHUNK), CHUNK)

    def near_copy(c):
        return remote(
            o_ref.at[:, rows_of(c), :],
            ext.at[pl.ds(2 * nz * odd, nz), rows_of(c), :],
            near_send.at[c], near_recv.at[c], {"space": near},
        )

    def near_arrival(c):
        spot = ext.at[pl.ds(near_slot, nz), rows_of(c), :]
        return remote(spot, spot, near_send.at[c], near_recv.at[c], {"space": near})

    def far_copy(c):
        return remote(
            ext.at[pl.ds(near_slot, nz), rows_of(c), :],
            ext.at[pl.ds(far_slot, nz), rows_of(c), :],
            far_send.at[c], far_recv.at[c], {"space": far},
        )

    def far_arrival(c):
        spot = ext.at[pl.ds(far_slot, nz), rows_of(c), :]
        return remote(spot, spot, far_send.at[c], far_recv.at[c], {"space": far})

    def block_rows(band, c):
        return pl.ds(pl.multiple_of(band * width + c * CHUNK, CHUNK), CHUNK)

    def chip_copy(d, c):
        spot = every.at[:, block_rows(b, c), :]
        return remote(spot, spot, chip_send.at[d - 1, c], chip_recv.at[d - 1, c], {"band": band_at(d)})

    def core_copy(c):
        spot = every.at[:, block_rows(b, c), :]
        return remote(spot, spot, core_send.at[c], core_recv.at[c], {"band": mate})

    def core_arrival(c):
        spot = every.at[:, block_rows(mate, c), :]
        return remote(spot, spot, core_send.at[c], core_recv.at[c], {"band": mate})

    def pass_copy(d, c):
        spot = every.at[:, block_rows(band_at(-d), c), :]
        return remote(spot, spot, pass_send.at[d - 1, c], pass_recv.at[d - 1, c], {"band": mate})

    def chip_arrival(d, c):
        spot = every.at[:, block_rows(band_at(-d), c), :]
        return remote(spot, spot, chip_send.at[d - 1, c], chip_recv.at[d - 1, c], {"band": band_at(-d)})

    def pass_arrival(d, c):
        other = band_at(-d) + 1 - 2 * core
        spot = every.at[:, block_rows(other, c), :]
        return remote(spot, spot, pass_send.at[d - 1, c], pass_recv.at[d - 1, c], {"band": mate})

    def take_chip(c):
        for d in range(1, chips):
            chip_arrival(d, c).wait_recv()
            pass_copy(d, c).start()

    near_copy(0).start()
    if chunks > 1:
        near_copy(1).start()
    own = pltpu.make_async_copy(o_ref, ext.at[pl.ds(nz, nz)], own_sem.at[0])
    own.start()
    fetch_p.wait()
    for i in range(nz):
        pot[nz + i] = p_ref[i : i + 1, :]
    mine = pot.at[pl.ds(nz, nz)]
    up = remote(mine, pot.at[pl.ds(0, nz)], pot_send.at[0], pot_recv.at[0], {"space": space_at(1)})
    down = remote(mine, pot.at[pl.ds(2 * nz, nz)], pot_send.at[1], pot_recv.at[1], {"space": space_at(-1)})
    up.start()
    down.start()
    fetch_m.wait()
    mh_ref[...], ml_ref[...] = split(m_ref[...])

    near_arrival(0).wait_recv()
    far_copy(0).start()
    near_copy(0).wait_send()
    if chunks > 2:
        near_copy(2).start()
    own.wait()
    up.wait_recv()
    down.wait_recv()

    along = [-0.5 * INV_SPACING2 * coef for coef in COEFS]

    def in_plane(slab):
        count = slab.shape[0]
        upper, lower = split(slab)
        both = plain_dot(jnp.concatenate([upper, lower], axis=0), mh_ref[...])
        return both[:count] + (both[count:] + plain_dot(upper, ml_ref[...]))

    def do_chunk(c, carry):
        rows = rows_of(c)

        @pl.when(c + 1 < chunks)
        def _():
            near_arrival(c + 1).wait_recv()
            far_copy(c + 1).start()
            near_copy(c + 1).wait_send()

        @pl.when(c + 3 < chunks)
        def _():
            near_copy(c + 3).start()

        far_arrival(c).wait_recv()

        wide = nz + 2 * REACH
        slab = ext[nz - REACH : 2 * nz + REACH, rows, :].reshape(wide * CHUNK, area)
        mixed[...] = in_plane(slab).reshape(wide, CHUNK, area)

        def first_plane(f, carry):
            q = f + (nz - REACH)
            total = mixed[f] + pot[q] * ext[q, rows, :]
            for k in range(REACH):
                total = total + along[k] * (ext[q + k + 1, rows, :] + ext[q - k - 1, rows, :])
            first[f] = total * (1.0 / HALF_SPAN)
            return carry

        lax.fori_loop(0, wide, first_plane, 0, unroll=4)

        slab = first[REACH : nz + REACH].reshape(nz * CHUNK, area)
        mixed[0:nz] = in_plane(slab).reshape(nz, CHUNK, area)

        def second_plane(j, carry):
            f = j + REACH
            total = mixed[j] + pot[j + nz] * first[f]
            for k in range(REACH):
                total = total + along[k] * (first[f + k + 1] + first[f - k - 1])
            every[j, block_rows(b, c), :] = total * (2.0 / HALF_SPAN) - ext[j + nz, rows, :]
            return carry

        lax.fori_loop(0, nz, second_plane, 0, unroll=4)

        for d in range(1, chips):
            chip_copy(d, c).start()
        core_copy(c).start()

        @pl.when(c >= 2)
        def _():
            take_chip(c - 2)

        return carry

    lax.fori_loop(0, chunks, do_chunk, 0)
    if chunks > 1:
        take_chip(chunks - 2)

    def each_chunk(action):
        def run(c, carry):
            action(c)
            return carry

        lax.fori_loop(0, chunks, run, 0)

    total_cols = nb * width
    slice_rows = width // n

    def gram(start, cols):
        def add(z, total):
            mine = every[z, pl.ds(pl.multiple_of(b * width, width), width), :]
            theirs = every[z, pl.ds(start, cols), :]
            return total + lax.dot_general(
                mine, theirs, (((1,), (1,)), ((), ())),
                precision=EXACT, preferred_element_type=jnp.float32,
            )

        total = lax.fori_loop(0, nz, add, jnp.zeros((width, cols), jnp.float32))
        for t in range(n):
            part[t, :, pl.ds(start, cols)] = total[t * slice_rows : (t + 1) * slice_rows, :]

    span = 2 * width
    staged = span % 128 == 0
    each_chunk(lambda c: core_arrival(c).wait_recv())
    if staged:
        gram(pl.multiple_of(chip * span, span), span)
    take_chip(chunks - 1)
    for d in range(1, chips):
        each_chunk(lambda c: pass_arrival(d, c).wait_recv())
        if staged:
            gram(pl.multiple_of(lax.rem(chip - d + chips, chips) * span, span), span)
    if not staged:
        gram(0, total_cols)
    save = pltpu.make_async_copy(every, every_out, out_sem.at[0])
    save.start()

    def rs_copy(d):
        t = space_at(d)
        return remote(part.at[t], inbox.at[d], rs_send.at[d], rs_recv.at[d], {"space": t})

    def ag_copy(d):
        spot = corr.at[b, s]
        return remote(spot, spot, ag_send.at[d], ag_recv.at[d], {"space": space_at(d)})

    def ag_arrival(d):
        spot = corr.at[b, space_at(-d)]
        return remote(spot, spot, ag_send.at[d], ag_recv.at[d], {"space": space_at(d)})

    for d in range(1, n):
        rs_copy(d).start()
    total = part[s]
    for d in range(1, n):
        rs_copy(d).wait_recv()
        total = total + inbox[d]
    corr[b, s] = total / cells
    for d in range(1, n):
        ag_copy(d).start()
    for d in range(1, n):
        ag_arrival(d).wait_recv()

    def cchip_copy(d):
        spot = corr.at[b]
        return remote(spot, spot, cchip_send.at[d - 1], cchip_recv.at[d - 1], {"band": band_at(d)})

    def cchip_arrival(d):
        spot = corr.at[band_at(-d)]
        return remote(spot, spot, cchip_send.at[d - 1], cchip_recv.at[d - 1], {"band": band_at(-d)})

    def cpass_copy(d):
        spot = corr.at[band_at(-d)]
        return remote(spot, spot, cpass_send.at[d - 1], cpass_recv.at[d - 1], {"band": mate})

    def cpass_arrival(d):
        spot = corr.at[band_at(-d) + 1 - 2 * core]
        return remote(spot, spot, cpass_send.at[d - 1], cpass_recv.at[d - 1], {"band": mate})

    ccore = remote(corr.at[b], corr.at[b], ccore_send, ccore_recv, {"band": mate})
    ccore_arrival = remote(corr.at[mate], corr.at[mate], ccore_send, ccore_recv, {"band": mate})
    for d in range(1, chips):
        cchip_copy(d).start()
    ccore.start()
    for d in range(1, chips):
        cchip_arrival(d).wait_recv()
        cpass_copy(d).start()
    ccore_arrival.wait_recv()
    for d in range(1, chips):
        cpass_arrival(d).wait_recv()
    store = pltpu.make_async_copy(corr, corr_out, out_sem.at[1])
    store.start()

    up.wait_send()
    down.wait_send()
    each_chunk(lambda c: far_copy(c).wait_send())
    each_chunk(lambda c: core_copy(c).wait_send())
    for d in range(1, chips):
        each_chunk(lambda c: chip_copy(d, c).wait_send())
        each_chunk(lambda c: pass_copy(d, c).wait_send())
        cchip_copy(d).wait_send()
        cpass_copy(d).wait_send()
    for d in range(1, n):
        rs_copy(d).wait_send()
        ag_copy(d).wait_send()
    ccore.wait_send()
    save.wait()
    store.wait()


def filter_and_correlate(orbitals, potential):
    nz, width, area = orbitals.shape
    n = lax.axis_size("space")
    nb = lax.axis_size("band")
    chunks = width // CHUNK
    chips = nb // 2
    slices = (nb, n, width // n, nb * width)
    dma = pltpu.SemaphoreType.DMA
    f32 = jnp.float32
    hops = max(chips - 1, 1)
    flops = 6 * 2 * nz * width * area * (3 * area + nb * width)
    every, corr = pl.pallas_call(
        functools.partial(filter_kernel, n, nb, float(nz * n * area)),
        out_shape=(
            jax.ShapeDtypeStruct((nz, nb * width, area), f32),
            jax.ShapeDtypeStruct(slices, f32),
        ),
        in_specs=[
            pl.BlockSpec(memory_space=pltpu.HBM),
            pl.BlockSpec(memory_space=pltpu.HBM),
            pl.BlockSpec(memory_space=pltpu.HBM),
        ],
        out_specs=(pl.BlockSpec(memory_space=pltpu.HBM), pl.BlockSpec(memory_space=pl.ANY)),
        scratch_shapes=[
            pltpu.VMEM((nz, area), f32),
            pltpu.VMEM((area, area), f32),
            pltpu.VMEM((area, area), jnp.bfloat16),
            pltpu.VMEM((area, area), jnp.bfloat16),
            pltpu.VMEM((3 * nz, width, area), f32),
            pltpu.VMEM((3 * nz, 1, area), f32),
            pltpu.VMEM((nz + 2 * REACH, CHUNK, area), f32),
            pltpu.VMEM((nz + 2 * REACH, CHUNK, area), f32),
            pltpu.VMEM((nz, nb * width, area), f32),
            pltpu.VMEM(slices[1:], f32),
            pltpu.VMEM(slices[1:], f32),
            pltpu.VMEM(slices, f32),
            dma((3,)), dma((2,)), dma((2,)),
            dma((chunks,)), dma((chunks,)), dma((chunks,)), dma((chunks,)),
            dma((hops, chunks)), dma((hops, chunks)),
            dma((chunks,)), dma((chunks,)),
            dma((hops, chunks)), dma((hops, chunks)),
            dma((n,)), dma((n,)), dma((n,)), dma((n,)),
            dma((hops,)), dma((hops,)), dma, dma, dma((hops,)), dma((hops,)), dma((2,)),
        ],
        compiler_params=pltpu.CompilerParams(
            collective_id=0, has_side_effects=True, vmem_limit_bytes=60 * 1024 * 1024
        ),
        cost_estimate=pl.CostEstimate(flops=flops, bytes_accessed=10 * 2**20, transcendentals=0),
    )(orbitals, potential, jnp.asarray(in_plane_matrix(area)))
    return every, corr.reshape(nb * width, nb * width)


def rotate_kernel(
    s_ref, every_ref, corr_out, out_ref, inverse, tile, spread, panel, every, rows, sems
):
    fetch = pltpu.make_async_copy(every_ref, every, sems.at[0])
    fetch.start()
    store = pltpu.make_async_copy(s_ref, corr_out, sems.at[1])
    store.start()
    inverse_factor_in(s_ref, inverse, tile, spread, panel)
    fetch.wait()
    nz, width, _ = out_ref.shape
    b = lax.axis_index("band")

    own = split(inverse[pl.ds(pl.multiple_of(b * width, width), width), :])
    rows[0:width] = own[0]
    rows[width : 2 * width] = own[1]

    def plane(z, carry):
        upper, lower = split(every[z])
        both = plain_dot(rows[...], upper)
        out_ref[z] = both[:width] + (both[width:] + plain_dot(rows[0:width], lower))
        return carry

    lax.fori_loop(0, nz, plane, 0)
    store.wait()


def factor_and_rotate(correlation, every, width):
    size = correlation.shape[0]
    nz, _, area = every.shape
    f32 = jnp.float32
    return pl.pallas_call(
        rotate_kernel,
        out_shape=(
            jax.ShapeDtypeStruct((size, size), f32),
            jax.ShapeDtypeStruct((nz, width, area), f32),
        ),
        in_specs=[pl.BlockSpec(memory_space=pltpu.VMEM), pl.BlockSpec(memory_space=pltpu.HBM)],
        out_specs=(pl.BlockSpec(memory_space=pl.ANY), pl.BlockSpec(memory_space=pltpu.VMEM)),
        scratch_shapes=[
            pltpu.VMEM((size, size), f32),
            pltpu.VMEM((BLOCK, BLOCK), f32),
            pltpu.VMEM((4 * ROWS * ROWS, BLOCK), f32),
            pltpu.VMEM((BLOCK, size), f32),
            pltpu.VMEM((nz, size, area), f32),
            pltpu.VMEM((2 * width, size), jnp.bfloat16),
            pltpu.SemaphoreType.DMA((2,)),
        ],
        compiler_params=pltpu.CompilerParams(vmem_limit_bytes=48 * 1024 * 1024),
    )(correlation, every)


def per_device(orbitals, potential):
    every, correlation = filter_and_correlate(orbitals, potential)
    correlation, rotated = factor_and_rotate(correlation, every, orbitals.shape[1])
    return (rotated, correlation)


def solution(mesh):
    return jax.shard_map(
        per_device,
        mesh=mesh,
        in_specs=(P("space", "band", None), P("space", None)),
        out_specs=(P("space", "band", None), P()),
        check_vma=False,
    )
```
